32 devices in a mesh: gene: 4 (over z), cell: 2 (over y), site: 4 (over x, core).
Axes of the slice: x: 2, y: 2, z: 4, core: 2. Of those that a mesh axis runs over, the one named last changes fastest.
Arguments:
- expr: bfloat16 [1024, 20000], P('cell', 'gene'), may hold values from -6 to 6
- proj_weight: bfloat16 [20000, 512], P('gene'), may hold values from -0.0390625 to 0.0390625
- centroids: bfloat16 [8192, 512], P('site'), may hold values from -6 to 6
- growth: float32 [1024], P('cell'), may hold values from 0.5 to 6
- site_weight: float32 [8192], P('site'), may hold values from 0.5 to 6
Outputs:
- cell_pot: float32 [1024], P('cell')
- site_pot: float32 [8192], P('site')
- barycenter: float32 [8192, 512], P('site')
The draws below stay inside these ranges and needn't reach their ends.
All inputs are finite; a program needn't handle non-finite values.
Results may differ from the reference program's by a relative error of at most 0.0033.
The reference program's roundings to bfloat16 on the way (of `projected` and `coupling`) count: a program that leaves them out, or rounds other values in their place, can miss the bound.
Values may be sent and summed in bfloat16 or wider, within the bound.
A program may use at most 64 MiB of HBM per device.

```python
import math
import jax
import jax.numpy as jnp
from jax import lax

G = 20000
K = 512
ROUNDS = 2
CELLS = 1024
SITES = 8192


def ramped(key, length):
    base = jnp.exp(jax.random.uniform(key, (length,), jnp.float32, math.log(0.5), math.log(2.0)))
    ramp = 1.0 + 2.0 * jnp.arange(length).astype(jnp.float32) / max(length - 1, 1)
    return base * ramp


def draw_growth(key, part):
    return ramped(jax.random.fold_in(key, 11), CELLS)


def draw_site_weight(key, part):
    return ramped(jax.random.fold_in(key, 23), SITES)


def levels(rng, extent, pieces, least, largest):
    level = 1.0
    for axis_at, parts in pieces:
        draws = jax.random.uniform(jax.random.fold_in(jax.random.fold_in(rng, 6), axis_at), (parts,), jnp.float32, least / len(pieces), largest / len(pieces))
        level = level * jnp.repeat(jnp.exp(draws), extent[axis_at] // parts).reshape((-1,) + (1,) * (len(extent) - 1 - axis_at))
    return level


def normal_values(own_key, shape, scale, reach, split=(), dtype=jnp.bfloat16):
    entries = jax.random.normal(own_key, shape, jnp.float32) * scale
    if len(split) > 0:
        entries = levels(own_key, shape, split, -0.22, 0.18) * entries
    return jnp.clip(entries, min=-reach, max=reach).astype(dtype)


def setup_inputs(seed: int = 0) -> dict:
    keys = jax.random.split(jax.random.key(seed), 6)
    return {
        "expr": normal_values(keys[0], (CELLS, G), 1.0, 6.0, ((0, 2), (1, 4))),
        "proj_weight": normal_values(keys[1], (G, K), G ** -0.5, 0.0390625, ((0, 4),)),
        "centroids": normal_values(keys[2], (SITES, K), 1.0, 6.0, ((0, 4),)),
        "growth": draw_growth(jax.random.fold_in(keys[5], 71), 0),
        "site_weight": draw_site_weight(jax.random.fold_in(keys[5], 71), 0),
    }


EPSILON = 0.02


def log_sum_exp(scores, axis_index):
    peak = jnp.max(scores, axis=axis_index, keepdims=True)
    summed = jnp.sum(jnp.exp(scores - peak), axis=axis_index)
    return jnp.squeeze(peak, axis_index) + jnp.log(summed)


def reference(expr, proj_weight, centroids, growth, site_weight):
    projected = jnp.dot(expr, proj_weight, preferred_element_type=jnp.float32).astype(jnp.bfloat16)
    proj_f = projected.astype(jnp.float32)
    cent_f = centroids.astype(jnp.float32)
    proj_norm = jnp.sum(proj_f * proj_f, axis=1) / K
    cent_norm = jnp.sum(cent_f * cent_f, axis=1) / K
    cross = lax.dot_general(projected, centroids, (((1,), (1,)), ((), ())), preferred_element_type=jnp.float32)
    distance = proj_norm[:, None] + cent_norm[None, :] - 2.0 * cross / K
    log_a = jnp.log(growth / jnp.sum(growth))
    site_share = site_weight / jnp.sum(site_weight)
    log_b = jnp.log(site_share)
    site_pot = jnp.zeros((SITES,), jnp.float32)
    cell_pot = jnp.zeros((CELLS,), jnp.float32)
    for turn in range(ROUNDS):
        cell_pot = EPSILON * log_a - EPSILON * log_sum_exp((site_pot[None, :] - distance) / EPSILON, 1)
        site_pot = EPSILON * log_b - EPSILON * log_sum_exp((cell_pot[:, None] - distance) / EPSILON, 0)
    coupling = jnp.exp((cell_pot[:, None] + site_pot[None, :] - distance) / EPSILON).astype(jnp.bfloat16)
    carried = lax.dot_general(coupling, projected, (((0,), (0,)), ((), ())), preferred_element_type=jnp.float32)
    barycenter = carried / site_share[:, None]
    return (cell_pot, site_pot, barycenter)
```

```python
import functools
import math

import jax
import jax.numpy as jnp
from jax import lax
from jax.experimental import pallas as pl
from jax.experimental.pallas import tpu as pltpu
from jax.sharding import PartitionSpec as P

ROUNDS = 2


EPSILON = 0.02


def merged(part, axis, combine):
    gathered = jax.tree.map(lambda a: lax.all_gather(a, axis), part)

    def take(source):
        return jax.tree.map(lambda a: lax.dynamic_index_in_dim(a, source, 0, False), gathered)

    return lax.fori_loop(
        1, lax.axis_size(axis), lambda source, state: combine(state, take(source)), take(0)
    )


def join_lse(first_pair, second_pair):
    peak = jnp.maximum(first_pair[0], second_pair[0])
    summed = first_pair[1] * jnp.exp(first_pair[0] - peak) + second_pair[1] * jnp.exp(
        second_pair[0] - peak
    )
    return (peak, summed)


def over_sites(scores):
    local_peak = jnp.max(scores, axis=1)
    local_sum = jnp.sum(jnp.exp(scores - local_peak[:, None]), axis=1)
    peak, summed = merged((local_peak, local_sum), "site", join_lse)
    return peak + jnp.log(summed)


def over_cells(scores):
    local_peak = jnp.max(scores, axis=0)
    local_sum = jnp.sum(jnp.exp(scores - local_peak[None, :]), axis=0)
    peak, summed = merged((local_peak, local_sum), "cell", join_lse)
    return peak + jnp.log(summed)


def shards(expr, proj_weight, centroids, growth, site_weight):
    cell_rows = expr.shape[0]
    features = proj_weight.shape[1]
    partial_term = jnp.dot(expr, proj_weight, preferred_element_type=jnp.float32)
    projected = lax.psum(partial_term, "gene").astype(jnp.bfloat16)
    proj_f = projected.astype(jnp.float32)
    cent_f = centroids.astype(jnp.float32)
    proj_norm = jnp.sum(proj_f * proj_f, axis=1) / features
    cent_norm = jnp.sum(cent_f * cent_f, axis=1) / features
    cross = lax.dot_general(
        projected, centroids, (((1,), (1,)), ((), ())), preferred_element_type=jnp.float32
    )
    distance = proj_norm[:, None] + cent_norm[None, :] - 2.0 * cross / features
    growth_total = lax.psum(jnp.sum(growth), "cell")
    weight_total = lax.psum(jnp.sum(site_weight), "site")
    log_a = jnp.log(growth / growth_total)
    site_share = site_weight / weight_total
    log_b = jnp.log(site_share)
    site_pot = jnp.zeros((centroids.shape[0],), jnp.float32)
    cell_pot = jnp.zeros((cell_rows,), jnp.float32)
    for turn in range(ROUNDS):
        cell_pot = EPSILON * log_a - EPSILON * over_sites((site_pot[None, :] - distance) / EPSILON)
        site_pot = EPSILON * log_b - EPSILON * over_cells((cell_pot[:, None] - distance) / EPSILON)
    coupling = jnp.exp((cell_pot[:, None] + site_pot[None, :] - distance) / EPSILON).astype(
        jnp.bfloat16
    )
    carried = lax.dot_general(
        coupling, projected, (((0,), (0,)), ((), ())), preferred_element_type=jnp.float32
    )
    summed = lax.psum(carried, "cell")
    barycenter = summed / site_share[:, None]
    return (cell_pot, site_pot, barycenter)


MESH = pl.DeviceIdType.MESH
LOG2E = 1.0 / math.log(2.0)
LN2 = math.log(2.0)
GENE, CELL, SITE = 4, 2, 4
LANES = 128
TALL = 256


def tiled(column, width):
    return jnp.concatenate([column] * (width // LANES), axis=1)


def diagonal():
    rows = lax.broadcasted_iota(jnp.int32, (LANES, LANES), 0)
    return rows == lax.broadcasted_iota(jnp.int32, (LANES, LANES), 1)


def to_column(row):
    spread = jnp.where(diagonal(), jnp.broadcast_to(row, (LANES, LANES)), 0.0)
    return jnp.broadcast_to(jnp.sum(spread, axis=1, keepdims=True), (LANES, LANES))


def to_row(column):
    return jnp.sum(jnp.where(diagonal(), column, 0.0), axis=0, keepdims=True)


def scaled_norms(block, scale):
    block = block.astype(jnp.float32)
    total = jnp.sum(block * block, axis=1, keepdims=True) * scale
    return jnp.broadcast_to(total, (block.shape[0], LANES))


def fold(scores_ref, pot, start, lane, state):
    peak, total = state
    block = scores_ref[pl.ds(start, TALL), lane * LANES : (lane + 1) * LANES]
    block = (block + pot).reshape(TALL // 8, 8, LANES)
    new_peak = jnp.maximum(peak, jnp.max(block, axis=0))
    total = total * jnp.exp2(peak - new_peak) + jnp.sum(jnp.exp2(block - new_peak[None]), axis=0)
    return new_peak, total


def close(state):
    peak, total = state
    top = jnp.max(peak, axis=0, keepdims=True)
    return top, jnp.sum(total * jnp.exp2(peak - top), axis=0, keepdims=True)


def prepare_kernel(
    part_ref, cent_hbm, growth_ref, weight_ref,
    proj_out, pot_out, cell_out, weight_out,
    cent, arrived, proj, scores, site_pot, log_share, grow, message,
    local_sem, reduce_send, reduce_recv, z_send, z_recv, x_send, x_recv, y_send, y_recv,
    diag_send, diag_recv, core_send, core_recv, grow_send, grow_recv, lse_send, lse_recv,
):
    gene, cell, site = lax.axis_index("gene"), lax.axis_index("cell"), lax.axis_index("site")
    cell_rows = growth_ref.shape[1]
    cells = CELL * cell_rows
    sites, features = cent.shape
    strip = cell_rows // SITE
    piece = strip // GENE
    other_cell = 1 - cell
    x_site = lax.rem(site + 2, SITE)
    core_site = site + 1 - 2 * lax.rem(site, 2)
    far_site = lax.rem(core_site + 2, SITE)
    genes = [gene] + [lax.rem(gene + d, GENE) for d in range(1, GENE)]
    back = [gene] + [lax.rem(gene + GENE - d, GENE) for d in range(1, GENE)]
    peers = [(genes[d], cell, site) for d in range(1, GENE)]
    x_dev, y_dev = (gene, cell, x_site), (gene, other_cell, site)
    core_dev, far_dev = (gene, cell, core_site), (gene, cell, far_site)
    site_devs = [(core_dev, core_site), (x_dev, x_site), (far_dev, far_site)]

    def remote(src, dst, send, recv, device):
        return pltpu.make_async_remote_copy(
            src_ref=src, dst_ref=dst, send_sem=send, recv_sem=recv,
            device_id=device, device_id_type=MESH,
        )

    load = pltpu.make_async_copy(cent_hbm, cent, local_sem)
    load.start()
    barrier = pltpu.get_barrier_semaphore()
    everyone = peers + [x_dev, y_dev, core_dev, far_dev]
    for device in everyone:
        pl.semaphore_signal(barrier, inc=1, device_id=device, device_id_type=MESH)
    pl.semaphore_wait(barrier, len(everyone))

    sent = []

    reduce = []
    for d in range(1, GENE):
        copy = remote(
            part_ref.at[pl.ds(pl.multiple_of(genes[d] * piece, piece), piece)],
            arrived.at[d - 1], reduce_send.at[d - 1], reduce_recv.at[d - 1], peers[d - 1],
        )
        copy.start()
        reduce.append(copy)
    grow[cell] = growth_ref[...]
    growth_copy = remote(grow.at[cell], grow.at[cell], grow_send, grow_recv, y_dev)
    growth_copy.start()

    norm_scale = LOG2E / (features * EPSILON)
    weight = weight_ref[...]
    load.wait()

    def norms(step, carry):
        start = pl.multiple_of(step * LANES, LANES)
        site_pot[pl.ds(start, LANES), :] = -scaled_norms(cent[pl.ds(start, LANES), :], norm_scale)
        log_share[pl.ds(start, LANES), :] = to_column(weight_ref[pl.ds(step, 1), :])
        return carry

    lax.fori_loop(0, sites // LANES, norms, 0)
    weight_sum = jnp.sum(jnp.sum(weight, axis=0, keepdims=True), axis=1, keepdims=True)
    weight_row = jnp.broadcast_to(weight_sum, (1, LANES))

    def rows(cell_at, site_at, gene_at):
        at = cell_at * cell_rows + site_at * strip + gene_at * piece
        return proj.at[pl.ds(pl.multiple_of(at, piece), piece)]

    def group(cell_at, site_at):
        at = cell_at * cell_rows + site_at * strip
        return proj.at[pl.ds(pl.multiple_of(at, strip), strip)]

    def send(ref, send_sem, recv_sem, device):
        copy = remote(ref, ref, send_sem, recv_sem, device)
        copy.start()
        sent.append(copy)

    def await_piece(ref, send_sem, recv_sem, device):
        remote(ref, ref, send_sem, recv_sem, device).wait_recv()

    total = part_ref[pl.ds(pl.multiple_of(gene * piece, piece), piece), :]
    for d in range(1, GENE):
        reduce[d - 1].wait_recv()
        total = total + arrived[d - 1]
    own_at = cell * cell_rows + site * strip + gene * piece
    proj[pl.ds(pl.multiple_of(own_at, piece), piece), :] = total.astype(jnp.bfloat16)

    for d in range(1, GENE):
        send(rows(cell, site, gene), z_send.at[d - 1], z_recv.at[d - 1], peers[d - 1])
    for d in range(GENE):
        block = rows(cell, site, back[d])
        if d > 0:
            await_piece(block, z_send.at[d - 1], z_recv.at[d - 1], peers[d - 1])
        send(block, x_send.at[d], x_recv.at[d], x_dev)
        send(block, y_send.at[d], y_recv.at[d], y_dev)
    send(group(cell, site), core_send.at[0], core_recv.at[0], core_dev)
    for d in range(GENE):
        block = rows(cell, x_site, back[d])
        await_piece(block, x_send.at[d], x_recv.at[d], x_dev)
        if d < 2:
            send(block, diag_send.at[d], diag_recv.at[d], y_dev)
        block = rows(other_cell, site, back[d])
        await_piece(block, y_send.at[d], y_recv.at[d], y_dev)
        if d >= 2:
            send(block, diag_send.at[d], diag_recv.at[d], x_dev)
    send(group(cell, x_site), core_send.at[1], core_recv.at[1], core_dev)
    send(group(other_cell, site), core_send.at[2], core_recv.at[2], core_dev)
    for d in range(GENE):
        await_piece(
            rows(other_cell, x_site, back[d]), diag_send.at[d], diag_recv.at[d],
            y_dev if d < 2 else x_dev,
        )
    send(group(other_cell, x_site), core_send.at[3], core_recv.at[3], core_dev)
    for at, (cell_at, site_at) in enumerate(
        ((cell, core_site), (cell, far_site), (other_cell, core_site), (other_cell, far_site))
    ):
        await_piece(group(cell_at, site_at), core_send.at[at], core_recv.at[at], core_dev)

    scale = 2.0 * norm_scale
    blocks = cells // LANES
    start_state = (
        jnp.full((8, LANES), -1e38, jnp.float32), jnp.zeros((8, LANES), jnp.float32)
    )

    def first(step, states):
        start = pl.multiple_of(step * TALL, TALL)
        scores[pl.ds(start, TALL), :] = scale * lax.dot_general(
            cent[pl.ds(start, TALL), :], proj[...], (((1,), (1,)), ((), ())),
            preferred_element_type=jnp.float32,
        )
        pot = site_pot[pl.ds(start, TALL), :]
        return tuple(fold(scores, pot, start, lane, states[lane]) for lane in range(blocks))

    states = lax.fori_loop(0, sites // TALL, first, (start_state,) * blocks)

    def exchange(turn, states):
        closed = [close(state) for state in states]
        peak = jnp.concatenate([pair[0] for pair in closed], axis=1)
        summed = jnp.concatenate([pair[1] for pair in closed], axis=1)
        message[turn, site] = jnp.concatenate([peak, summed, weight_row], axis=1)
        for at, (device, _) in enumerate(site_devs):
            own = message.at[turn, site]
            send(own, lse_send.at[turn, at], lse_recv.at[turn, at], device)
        for at, (device, source) in enumerate(site_devs):
            slot = message.at[turn, source]
            await_piece(slot, lse_send.at[turn, at], lse_recv.at[turn, at], device)
        parts = [message[turn, s] for s in range(SITE)]
        peak = functools.reduce(jnp.maximum, [part[:, :cells] for part in parts])
        summed = sum(part[:, cells : 2 * cells] * jnp.exp2(part[:, :cells] - peak) for part in parts)
        weight_total = sum(part[:, 2 * cells :] for part in parts)
        return peak + jnp.log(summed) * LOG2E, weight_total

    lse, weight_total = exchange(0, states)
    growth_copy.wait_send()
    slot = grow.at[other_cell]
    await_piece(slot, grow_send, grow_recv, y_dev)
    growth = jnp.concatenate([grow[c] for c in range(CELL)], axis=1)
    log_a = jnp.log(growth / jnp.sum(growth, axis=1, keepdims=True)) * LOG2E
    pot = log_a - lse

    rows_at_once = 32

    def second(step, states):
        start = pl.multiple_of(step * TALL, TALL)
        for sub in range(TALL // rows_at_once):
            at = pl.ds(start + sub * rows_at_once, rows_at_once)
            block = scores[at, :] + pot
            peak = jnp.max(block, axis=1, keepdims=True)
            summed = jnp.sum(jnp.exp2(block - peak), axis=1, keepdims=True)
            share = log_share[at, :] / weight_total
            site_pot[at, :] = jnp.log(share / summed) * LOG2E - peak
        new = site_pot[pl.ds(start, TALL), :]
        return tuple(fold(scores, new, start, lane, states[lane]) for lane in range(blocks))

    states = lax.fori_loop(0, sites // TALL, second, (start_state,) * blocks)
    lse, _ = exchange(1, states)
    pot = log_a - lse

    proj_out[...] = proj[...]
    pot_out[...] = pot
    weight_out[...] = weight_total
    own = proj[pl.ds(pl.multiple_of(cell * cell_rows, cell_rows), cell_rows), :].astype(jnp.float32)
    square = own * own
    high = square.astype(jnp.bfloat16)
    low = (square - high.astype(jnp.float32)).astype(jnp.bfloat16)
    ones = jnp.ones((16, features), jnp.bfloat16)
    norm = sum(
        lax.dot_general(ones, half, (((1,), (1,)), ((), ())), preferred_element_type=jnp.float32)
        for half in (high, low)
    )[:1]
    own_pot = jnp.where(cell == 0, pot[:, :cell_rows], pot[:, cell_rows:])
    cell_out[...] = (EPSILON * LN2) * own_pot + norm * (1.0 / features)
    for copy in sent:
        copy.wait_send()
    for copy in reduce:
        copy.wait_send()


def transport_kernel(
    cent_ref, proj_ref, pot_ref, cell_ref, weight_ref, total_ref, cell_out, site_out, bary_out
):
    features = cent_ref.shape[1]
    norm_scale = LOG2E / (features * EPSILON)
    cell_out[...] = cell_ref[...]
    pot = pot_ref[...]
    weight_total = total_ref[...]
    count = cent_ref.shape[0] // LANES
    for sub in range(count):
        at = pl.ds(sub * LANES, LANES)
        cent = cent_ref[at, :]
        block = (2.0 * norm_scale) * lax.dot_general(
            cent, proj_ref[...], (((1,), (1,)), ((), ())), preferred_element_type=jnp.float32
        )
        block = block + pot
        peak = jnp.max(block, axis=1, keepdims=True)
        block = jnp.exp2(block - peak)
        summed = jnp.sum(block, axis=1, keepdims=True)
        share = to_column(weight_ref[0, sub : sub + 1, :]) / weight_total
        ratio = share / summed
        site_pot = (EPSILON * LN2) * (jnp.log(ratio) * LOG2E - peak) + scaled_norms(
            cent, 1.0 / features
        )
        site_out[0, sub : sub + 1, :] = to_row(site_pot)
        coupling = (block * tiled(ratio, block.shape[1])).astype(jnp.bfloat16)
        carried = jnp.dot(coupling, proj_ref[...], preferred_element_type=jnp.float32)
        bary_out[at, :] = carried * tiled(1.0 / share, features)


def fused_shards(expr, proj_weight, centroids, growth, site_weight):
    cell_rows, genes = expr.shape
    sites, features = centroids.shape
    strip = cell_rows // SITE
    cells = CELL * cell_rows
    quarter = lax.dynamic_slice(expr, (lax.axis_index("site") * strip, 0), (strip, genes))
    part = jnp.dot(quarter, proj_weight, preferred_element_type=jnp.float32)
    vmem = pl.BlockSpec(memory_space=pltpu.VMEM)
    weight = site_weight.reshape(sites // LANES, LANES)
    dma = pltpu.SemaphoreType.DMA
    proj, pot, cell_pot, total = pl.pallas_call(
        prepare_kernel,
        out_shape=(
            jax.ShapeDtypeStruct((cells, features), jnp.bfloat16),
            jax.ShapeDtypeStruct((1, cells), jnp.float32),
            jax.ShapeDtypeStruct((1, cell_rows), jnp.float32),
            jax.ShapeDtypeStruct((1, LANES), jnp.float32),
        ),
        in_specs=[vmem, pl.BlockSpec(memory_space=pl.ANY), vmem, vmem],
        out_specs=(vmem,) * 4,
        scratch_shapes=[
            pltpu.VMEM((sites, features), jnp.bfloat16),
            pltpu.VMEM((GENE - 1, strip // GENE, features), jnp.float32),
            pltpu.VMEM((cells, features), jnp.bfloat16),
            pltpu.VMEM((sites, cells), jnp.float32),
            pltpu.VMEM((sites, LANES), jnp.float32),
            pltpu.VMEM((sites, LANES), jnp.float32),
            pltpu.VMEM((CELL, 1, cell_rows), jnp.float32),
            pltpu.VMEM((ROUNDS, SITE, 1, 2 * cells + LANES), jnp.float32),
            dma, dma((3,)), dma((3,)), dma((3,)), dma((3,)),
            dma((4,)), dma((4,)), dma((4,)), dma((4,)), dma((4,)), dma((4,)), dma((4,)), dma((4,)),
            dma, dma, dma((ROUNDS, 3)), dma((ROUNDS, 3)),
        ],
        compiler_params=pltpu.CompilerParams(
            collective_id=0, has_side_effects=True, vmem_limit_bytes=40 * 1024 * 1024
        ),
        name="prepare",
    )(part, centroids, growth.reshape(1, cell_rows), weight)
    tall = 512
    steps = sites // tall
    per = tall // LANES
    whole = lambda shape: pl.BlockSpec(shape, lambda i: (0,) * len(shape))
    cell_pot, site_pot, barycenter = pl.pallas_call(
        transport_kernel,
        grid=(steps,),
        out_shape=(
            jax.ShapeDtypeStruct((1, cell_rows), jnp.float32),
            jax.ShapeDtypeStruct((steps, per, LANES), jnp.float32),
            jax.ShapeDtypeStruct((sites, features), jnp.float32),
        ),
        in_specs=[
            pl.BlockSpec((tall, features), lambda i: (i, 0)),
            whole((cells, features)),
            whole((1, cells)),
            whole((1, cell_rows)),
            pl.BlockSpec((1, per, LANES), lambda i: (i, 0, 0)),
            whole((1, LANES)),
        ],
        out_specs=(
            whole((1, cell_rows)),
            pl.BlockSpec((1, per, LANES), lambda i: (i, 0, 0)),
            pl.BlockSpec((tall, features), lambda i: (i, 0)),
        ),
        compiler_params=pltpu.CompilerParams(vmem_limit_bytes=40 * 1024 * 1024),
        name="transport",
    )(centroids, proj, pot, cell_pot, weight.reshape(steps, per, LANES), total)
    return cell_pot.reshape(cell_rows), site_pot.reshape(sites), barycenter


def solution(mesh):
    placed = (P("cell", "gene"), P("gene", None), P("site", None), P("cell"), P("site"))
    sizes = dict(mesh.shape)
    small = sizes["gene"] == 4 and sizes["cell"] == 2 and sizes["site"] == 4
    return jax.shard_map(
        fused_shards if small else shards,
        mesh=mesh,
        in_specs=placed,
        out_specs=(P("cell"), P("site"), P("site", None)),
        check_vma=False,
    )
```

```python
import functools
import math

import jax
import jax.numpy as jnp
from jax import lax
from jax.experimental import pallas as pl
from jax.experimental.pallas import tpu as pltpu
from jax.sharding import PartitionSpec as P

ROUNDS = 2


EPSILON = 0.02


def merged(part, axis, combine):
    gathered = jax.tree.map(lambda a: lax.all_gather(a, axis), part)

    def take(source):
        return jax.tree.map(lambda a: lax.dynamic_index_in_dim(a, source, 0, False), gathered)

    return lax.fori_loop(
        1, lax.axis_size(axis), lambda source, state: combine(state, take(source)), take(0)
    )


def join_lse(first_pair, second_pair):
    peak = jnp.maximum(first_pair[0], second_pair[0])
    summed = first_pair[1] * jnp.exp(first_pair[0] - peak) + second_pair[1] * jnp.exp(
        second_pair[0] - peak
    )
    return (peak, summed)


def over_sites(scores):
    local_peak = jnp.max(scores, axis=1)
    local_sum = jnp.sum(jnp.exp(scores - local_peak[:, None]), axis=1)
    peak, summed = merged((local_peak, local_sum), "site", join_lse)
    return peak + jnp.log(summed)


def over_cells(scores):
    local_peak = jnp.max(scores, axis=0)
    local_sum = jnp.sum(jnp.exp(scores - local_peak[None, :]), axis=0)
    peak, summed = merged((local_peak, local_sum), "cell", join_lse)
    return peak + jnp.log(summed)


def shards(expr, proj_weight, centroids, growth, site_weight):
    cell_rows = expr.shape[0]
    features = proj_weight.shape[1]
    partial_term = jnp.dot(expr, proj_weight, preferred_element_type=jnp.float32)
    projected = lax.psum(partial_term, "gene").astype(jnp.bfloat16)
    proj_f = projected.astype(jnp.float32)
    cent_f = centroids.astype(jnp.float32)
    proj_norm = jnp.sum(proj_f * proj_f, axis=1) / features
    cent_norm = jnp.sum(cent_f * cent_f, axis=1) / features
    cross = lax.dot_general(
        projected, centroids, (((1,), (1,)), ((), ())), preferred_element_type=jnp.float32
    )
    distance = proj_norm[:, None] + cent_norm[None, :] - 2.0 * cross / features
    growth_total = lax.psum(jnp.sum(growth), "cell")
    weight_total = lax.psum(jnp.sum(site_weight), "site")
    log_a = jnp.log(growth / growth_total)
    site_share = site_weight / weight_total
    log_b = jnp.log(site_share)
    site_pot = jnp.zeros((centroids.shape[0],), jnp.float32)
    cell_pot = jnp.zeros((cell_rows,), jnp.float32)
    for turn in range(ROUNDS):
        cell_pot = EPSILON * log_a - EPSILON * over_sites((site_pot[None, :] - distance) / EPSILON)
        site_pot = EPSILON * log_b - EPSILON * over_cells((cell_pot[:, None] - distance) / EPSILON)
    coupling = jnp.exp((cell_pot[:, None] + site_pot[None, :] - distance) / EPSILON).astype(
        jnp.bfloat16
    )
    carried = lax.dot_general(
        coupling, projected, (((0,), (0,)), ((), ())), preferred_element_type=jnp.float32
    )
    summed = lax.psum(carried, "cell")
    barycenter = summed / site_share[:, None]
    return (cell_pot, site_pot, barycenter)


MESH = pl.DeviceIdType.MESH
LOG2E = 1.0 / math.log(2.0)
LN2 = math.log(2.0)
GENE, CELL, SITE = 4, 2, 4
LANES = 128
TALL = 256


def tiled(column, width):
    return jnp.concatenate([column] * (width // LANES), axis=1)


def diagonal():
    rows = lax.broadcasted_iota(jnp.int32, (LANES, LANES), 0)
    return rows == lax.broadcasted_iota(jnp.int32, (LANES, LANES), 1)


def to_column(row):
    spread = jnp.where(diagonal(), jnp.broadcast_to(row, (LANES, LANES)), 0.0)
    return jnp.broadcast_to(jnp.sum(spread, axis=1, keepdims=True), (LANES, LANES))


def to_row(column):
    return jnp.sum(jnp.where(diagonal(), column, 0.0), axis=0, keepdims=True)


def scaled_norms(block, scale):
    block = block.astype(jnp.float32)
    total = jnp.sum(block * block, axis=1, keepdims=True) * scale
    return jnp.broadcast_to(total, (block.shape[0], LANES))


def fold(scores_ref, pot, start, lane_start, state):
    peak, total = state
    block = scores_ref[pl.ds(start, TALL), pl.ds(lane_start, LANES)]
    block = (block + pot).reshape(TALL // 8, 8, LANES)
    new_peak = jnp.maximum(peak, jnp.max(block, axis=0))
    total = total * jnp.exp2(peak - new_peak) + jnp.sum(jnp.exp2(block - new_peak[None]), axis=0)
    return new_peak, total


def close(state):
    peak, total = state
    top = jnp.max(peak, axis=0, keepdims=True)
    return top, jnp.sum(total * jnp.exp2(peak - top), axis=0, keepdims=True)


def prepare_kernel(
    part_ref, cent_hbm, growth_ref, weight_ref,
    proj_out, pot_out, cell_out, weight_out, scores, weight_col, norm_out,
    cent, arrived, proj, site_pot, grow, message,
    local_sem, reduce_send, reduce_recv, z_send, z_recv, x_send, x_recv, y_send, y_recv,
    diag_send, diag_recv, core_send, core_recv, grow_send, grow_recv, lse_send, lse_recv,
):
    gene, cell, site = lax.axis_index("gene"), lax.axis_index("cell"), lax.axis_index("site")
    cell_rows = growth_ref.shape[1]
    cells = CELL * cell_rows
    sites, features = cent.shape
    strip = cell_rows // SITE
    piece = strip // GENE
    other_cell = 1 - cell
    x_site = lax.rem(site + 2, SITE)
    core_site = site + 1 - 2 * lax.rem(site, 2)
    far_site = lax.rem(core_site + 2, SITE)
    genes = [gene] + [lax.rem(gene + d, GENE) for d in range(1, GENE)]
    back = [gene] + [lax.rem(gene + GENE - d, GENE) for d in range(1, GENE)]
    peers = [(genes[d], cell, site) for d in range(1, GENE)]
    x_dev, y_dev = (gene, cell, x_site), (gene, other_cell, site)
    core_dev, far_dev = (gene, cell, core_site), (gene, cell, far_site)
    site_devs = [(core_dev, core_site), (x_dev, x_site), (far_dev, far_site)]

    def remote(src, dst, send, recv, device):
        return pltpu.make_async_remote_copy(
            src_ref=src, dst_ref=dst, send_sem=send, recv_sem=recv,
            device_id=device, device_id_type=MESH,
        )

    load = pltpu.make_async_copy(cent_hbm, cent, local_sem)
    load.start()
    barrier = pltpu.get_barrier_semaphore()
    everyone = peers + [x_dev, y_dev, core_dev, far_dev]
    for device in everyone:
        pl.semaphore_signal(barrier, inc=1, device_id=device, device_id_type=MESH)
    pl.semaphore_wait(barrier, len(everyone))

    sent = []

    reduce = []
    for d in range(1, GENE):
        copy = remote(
            part_ref.at[pl.ds(pl.multiple_of(genes[d] * piece, piece), piece)],
            arrived.at[d - 1], reduce_send.at[d - 1], reduce_recv.at[d - 1], peers[d - 1],
        )
        copy.start()
        reduce.append(copy)
    grow[cell] = growth_ref[...]
    growth_copy = remote(grow.at[cell], grow.at[cell], grow_send, grow_recv, y_dev)
    growth_copy.start()

    norm_scale = LOG2E / (features * EPSILON)
    weight = weight_ref[...]
    load.wait()

    def norms(step, carry):
        start = pl.multiple_of(step * LANES, LANES)
        norm = scaled_norms(cent[pl.ds(start, LANES), :], norm_scale)
        site_pot[pl.ds(start, LANES), :] = -norm
        norm_out[pl.ds(step, 1), :] = to_row(norm)
        weight_col[pl.ds(start, LANES), :] = to_column(weight_ref[pl.ds(step, 1), :])
        return carry

    lax.fori_loop(0, sites // LANES, norms, 0)
    weight_sum = jnp.sum(jnp.sum(weight, axis=0, keepdims=True), axis=1, keepdims=True)
    weight_row = jnp.broadcast_to(weight_sum, (1, LANES))

    def rows(cell_at, site_at, gene_at):
        at = cell_at * cell_rows + site_at * strip + gene_at * piece
        return proj.at[pl.ds(pl.multiple_of(at, piece), piece)]

    def group(cell_at, site_at):
        at = cell_at * cell_rows + site_at * strip
        return proj.at[pl.ds(pl.multiple_of(at, strip), strip)]

    def send(ref, send_sem, recv_sem, device):
        copy = remote(ref, ref, send_sem, recv_sem, device)
        copy.start()
        sent.append(copy)

    def await_piece(ref, send_sem, recv_sem, device):
        remote(ref, ref, send_sem, recv_sem, device).wait_recv()

    total = part_ref[pl.ds(pl.multiple_of(gene * piece, piece), piece), :]
    for d in range(1, GENE):
        reduce[d - 1].wait_recv()
        total = total + arrived[d - 1]
    own_at = cell * cell_rows + site * strip + gene * piece
    proj[pl.ds(pl.multiple_of(own_at, piece), piece), :] = total.astype(jnp.bfloat16)

    for d in range(1, GENE):
        send(rows(cell, site, gene), z_send.at[d - 1], z_recv.at[d - 1], peers[d - 1])
    for d in range(GENE):
        block = rows(cell, site, back[d])
        if d > 0:
            await_piece(block, z_send.at[d - 1], z_recv.at[d - 1], peers[d - 1])
        send(block, x_send.at[d], x_recv.at[d], x_dev)
        send(block, y_send.at[d], y_recv.at[d], y_dev)
    send(group(cell, site), core_send.at[0], core_recv.at[0], core_dev)
    for d in range(GENE):
        block = rows(cell, x_site, back[d])
        await_piece(block, x_send.at[d], x_recv.at[d], x_dev)
        if d < 2:
            send(block, diag_send.at[d], diag_recv.at[d], y_dev)
        block = rows(other_cell, site, back[d])
        await_piece(block, y_send.at[d], y_recv.at[d], y_dev)
        if d >= 2:
            send(block, diag_send.at[d], diag_recv.at[d], x_dev)
    send(group(cell, x_site), core_send.at[1], core_recv.at[1], core_dev)
    send(group(other_cell, site), core_send.at[2], core_recv.at[2], core_dev)
    scale = 2.0 * norm_scale
    blocks = cells // LANES
    half_blocks = cell_rows // LANES
    bulk = 1024
    start_state = (
        jnp.full((8, LANES), -1e38, jnp.float32), jnp.zeros((8, LANES), jnp.float32)
    )

    def await_groups(pairs):
        for at, cell_at, site_at in pairs:
            await_piece(group(cell_at, site_at), core_send.at[at], core_recv.at[at], core_dev)

    def first(cell_at, start, states):
        side = pl.multiple_of(cell_at * cell_rows, cell_rows)
        scores[start : start + bulk, pl.ds(side, cell_rows)] = scale * lax.dot_general(
            cent[start : start + bulk, :], proj[pl.ds(side, cell_rows), :],
            (((1,), (1,)), ((), ())), preferred_element_type=jnp.float32,
        )

        def add(step, states):
            at = pl.multiple_of(start + step * TALL, TALL)
            pot = site_pot[pl.ds(at, TALL), :]
            return tuple(
                fold(scores, pot, at, pl.multiple_of(side + lane * LANES, LANES), states[lane])
                for lane in range(half_blocks)
            )

        return lax.fori_loop(0, bulk // TALL, add, states)

    await_groups(((0, cell, core_site), (1, cell, far_site)))
    here = first(cell, 0, (start_state,) * half_blocks)
    for d in range(GENE):
        await_piece(
            rows(other_cell, x_site, back[d]), diag_send.at[d], diag_recv.at[d],
            y_dev if d < 2 else x_dev,
        )
    send(group(other_cell, x_site), core_send.at[3], core_recv.at[3], core_dev)
    for start in range(bulk, sites, bulk):
        here = first(cell, start, here)
    await_groups(((2, other_cell, core_site), (3, other_cell, far_site)))
    there = (start_state,) * half_blocks
    for start in range(0, sites, bulk):
        there = first(other_cell, start, there)
    is_low = cell == 0
    pick = functools.partial(jax.tree.map, lambda p, q: jnp.where(is_low, p, q))
    states = pick(here, there) + pick(there, here)

    def exchange(turn, states):
        closed = [close(state) for state in states]
        peak = jnp.concatenate([pair[0] for pair in closed], axis=1)
        summed = jnp.concatenate([pair[1] for pair in closed], axis=1)
        message[turn, site] = jnp.concatenate([peak, summed, weight_row], axis=1)
        for at, (device, _) in enumerate(site_devs):
            own = message.at[turn, site]
            send(own, lse_send.at[turn, at], lse_recv.at[turn, at], device)
        for at, (device, source) in enumerate(site_devs):
            slot = message.at[turn, source]
            await_piece(slot, lse_send.at[turn, at], lse_recv.at[turn, at], device)
        parts = [message[turn, s] for s in range(SITE)]
        peak = functools.reduce(jnp.maximum, [part[:, :cells] for part in parts])
        summed = sum(part[:, cells : 2 * cells] * jnp.exp2(part[:, :cells] - peak) for part in parts)
        weight_total = sum(part[:, 2 * cells :] for part in parts)
        return peak + jnp.log(summed) * LOG2E, weight_total

    lse, weight_total = exchange(0, states)
    growth_copy.wait_send()
    slot = grow.at[other_cell]
    await_piece(slot, grow_send, grow_recv, y_dev)
    growth = jnp.concatenate([grow[c] for c in range(CELL)], axis=1)
    log_a = jnp.log(growth / jnp.sum(growth, axis=1, keepdims=True)) * LOG2E
    pot = log_a - lse

    rows_at_once = 32

    def second(step, states):
        start = pl.multiple_of(step * TALL, TALL)
        for sub in range(TALL // rows_at_once):
            at = pl.ds(start + sub * rows_at_once, rows_at_once)
            block = scores[at, :] + pot
            peak = jnp.max(block, axis=1, keepdims=True)
            summed = jnp.sum(jnp.exp2(block - peak), axis=1, keepdims=True)
            share = weight_col[at, :] / weight_total
            site_pot[at, :] = jnp.log(share / summed) * LOG2E - peak
        new = site_pot[pl.ds(start, TALL), :]
        return tuple(fold(scores, new, start, lane * LANES, states[lane]) for lane in range(blocks))

    states = lax.fori_loop(0, sites // TALL, second, (start_state,) * blocks)
    lse, _ = exchange(1, states)
    pot = log_a - lse

    proj_out[...] = proj[...]
    pot_out[...] = pot
    weight_out[...] = weight_total
    own = proj[pl.ds(pl.multiple_of(cell * cell_rows, cell_rows), cell_rows), :].astype(jnp.float32)
    square = own * own
    high = square.astype(jnp.bfloat16)
    low = (square - high.astype(jnp.float32)).astype(jnp.bfloat16)
    ones = jnp.ones((16, features), jnp.bfloat16)
    norm = sum(
        lax.dot_general(ones, half, (((1,), (1,)), ((), ())), preferred_element_type=jnp.float32)
        for half in (high, low)
    )[:1]
    own_pot = jnp.where(cell == 0, pot[:, :cell_rows], pot[:, cell_rows:])
    cell_out[...] = (EPSILON * LN2) * own_pot + norm * (1.0 / features)
    for copy in sent:
        copy.wait_send()
    for copy in reduce:
        copy.wait_send()


def transport_kernel(
    scores, proj, pot_ref, cell_ref, weight_col, total_ref, norm_ref,
    cell_out, site_out, bary_hbm, coupling, bary, sems,
):
    sites, features = bary.shape
    cells = scores.shape[1]
    rows_at_once = 32
    cell_out[...] = cell_ref[...]
    pot = pot_ref[...]
    weight_total = total_ref[...]

    def couple(chunk):
        slot = chunk % 2
        for base in range(0, TALL, LANES):
            columns = []
            for sub in range(base, base + LANES, rows_at_once):
                at = pl.ds(chunk * TALL + sub, rows_at_once)
                block = scores[at, :] + pot
                peak = jnp.max(block, axis=1, keepdims=True)
                block = jnp.exp2(block - peak)
                summed = jnp.sum(block, axis=1, keepdims=True)
                ratio = weight_col[at, :] / weight_total / summed
                columns.append(jnp.log(ratio) * LOG2E - peak)
                coupling[slot, sub : sub + rows_at_once, :] = (
                    block * tiled(ratio, cells)
                ).astype(jnp.bfloat16)
            row = (chunk * TALL + base) // LANES
            pot_row = to_row(jnp.concatenate(columns, axis=0))
            site_out[row : row + 1, :] = (EPSILON * LN2) * (pot_row + norm_ref[row : row + 1, :])

    def carry(chunk):
        at = pl.ds(chunk * TALL, TALL)
        carried = jnp.dot(coupling[chunk % 2], proj[...], preferred_element_type=jnp.float32)
        bary[at, :] = carried * tiled(weight_total / weight_col[at, :], features)
        copy = pltpu.make_async_copy(bary.at[at], bary_hbm.at[at], sems.at[chunk])
        copy.start()
        return copy

    copies = []
    chunks = sites // TALL
    couple(0)
    for chunk in range(chunks):
        if chunk + 1 < chunks:
            couple(chunk + 1)
        copies.append(carry(chunk))
    for copy in copies:
        copy.wait()


def fused_shards(expr, proj_weight, centroids, growth, site_weight):
    cell_rows, genes = expr.shape
    sites, features = centroids.shape
    strip = cell_rows // SITE
    cells = CELL * cell_rows
    quarter = lax.dynamic_slice(expr, (lax.axis_index("site") * strip, 0), (strip, genes))
    part = jnp.dot(quarter, proj_weight, preferred_element_type=jnp.float32)
    vmem = pl.BlockSpec(memory_space=pltpu.VMEM)
    weight = site_weight.reshape(sites // LANES, LANES)
    dma = pltpu.SemaphoreType.DMA
    proj, pot, cell_pot, total, scores, weight_col, norm = pl.pallas_call(
        prepare_kernel,
        out_shape=(
            jax.ShapeDtypeStruct((cells, features), jnp.bfloat16),
            jax.ShapeDtypeStruct((1, cells), jnp.float32),
            jax.ShapeDtypeStruct((1, cell_rows), jnp.float32),
            jax.ShapeDtypeStruct((1, LANES), jnp.float32),
            jax.ShapeDtypeStruct((sites, cells), jnp.float32),
            jax.ShapeDtypeStruct((sites, LANES), jnp.float32),
            jax.ShapeDtypeStruct((sites // LANES, LANES), jnp.float32),
        ),
        in_specs=[vmem, pl.BlockSpec(memory_space=pl.ANY), vmem, vmem],
        out_specs=(vmem,) * 7,
        scratch_shapes=[
            pltpu.VMEM((sites, features), jnp.bfloat16),
            pltpu.VMEM((GENE - 1, strip // GENE, features), jnp.float32),
            pltpu.VMEM((cells, features), jnp.bfloat16),
            pltpu.VMEM((sites, LANES), jnp.float32),
            pltpu.VMEM((CELL, 1, cell_rows), jnp.float32),
            pltpu.VMEM((ROUNDS, SITE, 1, 2 * cells + LANES), jnp.float32),
            dma, dma((3,)), dma((3,)), dma((3,)), dma((3,)),
            dma((4,)), dma((4,)), dma((4,)), dma((4,)), dma((4,)), dma((4,)), dma((4,)), dma((4,)),
            dma, dma, dma((ROUNDS, 3)), dma((ROUNDS, 3)),
        ],
        compiler_params=pltpu.CompilerParams(
            collective_id=0, has_side_effects=True, vmem_limit_bytes=36 * 1024 * 1024
        ),
        name="prepare",
    )(part, centroids, growth.reshape(1, cell_rows), weight)
    cell_pot, site_pot, barycenter = pl.pallas_call(
        transport_kernel,
        out_shape=(
            jax.ShapeDtypeStruct((1, cell_rows), jnp.float32),
            jax.ShapeDtypeStruct((sites // LANES, LANES), jnp.float32),
            jax.ShapeDtypeStruct((sites, features), jnp.float32),
        ),
        in_specs=[vmem] * 7,
        out_specs=(vmem, vmem, pl.BlockSpec(memory_space=pl.ANY)),
        scratch_shapes=[
            pltpu.VMEM((2, TALL, cells), jnp.bfloat16),
            pltpu.VMEM((sites, features), jnp.float32),
            dma((sites // TALL,)),
        ],
        compiler_params=pltpu.CompilerParams(vmem_limit_bytes=36 * 1024 * 1024),
        name="transport",
    )(scores, proj, pot, cell_pot, weight_col, total, norm)
    return cell_pot.reshape(cell_rows), site_pot.reshape(sites), barycenter


def solution(mesh):
    placed = (P("cell", "gene"), P("gene", None), P("site", None), P("cell"), P("site"))
    sizes = dict(mesh.shape)
    small = sizes["gene"] == 4 and sizes["cell"] == 2 and sizes["site"] == 4
    return jax.shard_map(
        fused_shards if small else shards,
        mesh=mesh,
        in_specs=placed,
        out_specs=(P("cell"), P("site"), P("site", None)),
        check_vma=False,
    )
```

```python
import functools
import math

import jax
import jax.numpy as jnp
from jax import lax
from jax.experimental import pallas as pl
from jax.experimental.pallas import tpu as pltpu
from jax.sharding import PartitionSpec as P

ROUNDS = 2


EPSILON = 0.02


def merged(part, axis, combine):
    gathered = jax.tree.map(lambda a: lax.all_gather(a, axis), part)

    def take(source):
        return jax.tree.map(lambda a: lax.dynamic_index_in_dim(a, source, 0, False), gathered)

    return lax.fori_loop(
        1, lax.axis_size(axis), lambda source, state: combine(state, take(source)), take(0)
    )


def join_lse(first_pair, second_pair):
    peak = jnp.maximum(first_pair[0], second_pair[0])
    summed = first_pair[1] * jnp.exp(first_pair[0] - peak) + second_pair[1] * jnp.exp(
        second_pair[0] - peak
    )
    return (peak, summed)


def over_sites(scores):
    local_peak = jnp.max(scores, axis=1)
    local_sum = jnp.sum(jnp.exp(scores - local_peak[:, None]), axis=1)
    peak, summed = merged((local_peak, local_sum), "site", join_lse)
    return peak + jnp.log(summed)


def over_cells(scores):
    local_peak = jnp.max(scores, axis=0)
    local_sum = jnp.sum(jnp.exp(scores - local_peak[None, :]), axis=0)
    peak, summed = merged((local_peak, local_sum), "cell", join_lse)
    return peak + jnp.log(summed)


def shards(expr, proj_weight, centroids, growth, site_weight):
    cell_rows = expr.shape[0]
    features = proj_weight.shape[1]
    partial_term = jnp.dot(expr, proj_weight, preferred_element_type=jnp.float32)
    projected = lax.psum(partial_term, "gene").astype(jnp.bfloat16)
    proj_f = projected.astype(jnp.float32)
    cent_f = centroids.astype(jnp.float32)
    proj_norm = jnp.sum(proj_f * proj_f, axis=1) / features
    cent_norm = jnp.sum(cent_f * cent_f, axis=1) / features
    cross = lax.dot_general(
        projected, centroids, (((1,), (1,)), ((), ())), preferred_element_type=jnp.float32
    )
    distance = proj_norm[:, None] + cent_norm[None, :] - 2.0 * cross / features
    growth_total = lax.psum(jnp.sum(growth), "cell")
    weight_total = lax.psum(jnp.sum(site_weight), "site")
    log_a = jnp.log(growth / growth_total)
    site_share = site_weight / weight_total
    log_b = jnp.log(site_share)
    site_pot = jnp.zeros((centroids.shape[0],), jnp.float32)
    cell_pot = jnp.zeros((cell_rows,), jnp.float32)
    for turn in range(ROUNDS):
        cell_pot = EPSILON * log_a - EPSILON * over_sites((site_pot[None, :] - distance) / EPSILON)
        site_pot = EPSILON * log_b - EPSILON * over_cells((cell_pot[:, None] - distance) / EPSILON)
    coupling = jnp.exp((cell_pot[:, None] + site_pot[None, :] - distance) / EPSILON).astype(
        jnp.bfloat16
    )
    carried = lax.dot_general(
        coupling, projected, (((0,), (0,)), ((), ())), preferred_element_type=jnp.float32
    )
    summed = lax.psum(carried, "cell")
    barycenter = summed / site_share[:, None]
    return (cell_pot, site_pot, barycenter)


MESH = pl.DeviceIdType.MESH
LOG2E = 1.0 / math.log(2.0)
LN2 = math.log(2.0)
GENE, CELL, SITE = 4, 2, 4
LANES = 128
TALL = 256


def tiled(column, width):
    return jnp.concatenate([column] * (width // LANES), axis=1)


def diagonal():
    rows = lax.broadcasted_iota(jnp.int32, (LANES, LANES), 0)
    return rows == lax.broadcasted_iota(jnp.int32, (LANES, LANES), 1)


def to_column(row):
    spread = jnp.where(diagonal(), jnp.broadcast_to(row, (LANES, LANES)), 0.0)
    return jnp.broadcast_to(jnp.sum(spread, axis=1, keepdims=True), (LANES, LANES))


def to_row(column):
    return jnp.sum(jnp.where(diagonal(), column, 0.0), axis=0, keepdims=True)


def scaled_norms(block, scale):
    block = block.astype(jnp.float32)
    total = jnp.sum(block * block, axis=1, keepdims=True) * scale
    return jnp.broadcast_to(total, (block.shape[0], LANES))


def fold(scores_ref, pot, start, lane_start, state):
    peak, total = state
    block = scores_ref[pl.ds(start, TALL), pl.ds(lane_start, LANES)]
    block = (block + pot).reshape(TALL // 8, 8, LANES)
    new_peak = jnp.maximum(peak, jnp.max(block, axis=0))
    total = total * jnp.exp2(peak - new_peak) + jnp.sum(jnp.exp2(block - new_peak[None]), axis=0)
    return new_peak, total


def close(state):
    peak, total = state
    top = jnp.max(peak, axis=0, keepdims=True)
    return top, jnp.sum(total * jnp.exp2(peak - top), axis=0, keepdims=True)


def prepare_kernel(
    part_ref, cent_hbm, growth_ref, weight_ref,
    proj_out, pot_out, cell_out, weight_out, scores, weight_col, norm_out,
    cent, arrived, proj, site_pot, grow, message,
    local_sem, reduce_send, reduce_recv, z_send, z_recv, x_send, x_recv, y_send, y_recv,
    diag_send, diag_recv, core_send, core_recv, grow_send, grow_recv, lse_send, lse_recv,
):
    gene, cell, site = lax.axis_index("gene"), lax.axis_index("cell"), lax.axis_index("site")
    cell_rows = growth_ref.shape[1]
    cells = CELL * cell_rows
    sites, features = cent.shape
    strip = cell_rows // SITE
    piece = strip // GENE
    other_cell = 1 - cell
    x_site = lax.rem(site + 2, SITE)
    core_site = site + 1 - 2 * lax.rem(site, 2)
    far_site = lax.rem(core_site + 2, SITE)
    genes = [gene] + [lax.rem(gene + d, GENE) for d in range(1, GENE)]
    back = [gene] + [lax.rem(gene + GENE - d, GENE) for d in range(1, GENE)]
    peers = [(genes[d], cell, site) for d in range(1, GENE)]
    x_dev, y_dev = (gene, cell, x_site), (gene, other_cell, site)
    core_dev, far_dev = (gene, cell, core_site), (gene, cell, far_site)
    site_devs = [(core_dev, core_site), (x_dev, x_site), (far_dev, far_site)]

    def remote(src, dst, send, recv, device):
        return pltpu.make_async_remote_copy(
            src_ref=src, dst_ref=dst, send_sem=send, recv_sem=recv,
            device_id=device, device_id_type=MESH,
        )

    load = pltpu.make_async_copy(cent_hbm, cent, local_sem)
    load.start()
    barrier = pltpu.get_barrier_semaphore()
    everyone = peers + [x_dev, y_dev, core_dev, far_dev]
    for device in everyone:
        pl.semaphore_signal(barrier, inc=1, device_id=device, device_id_type=MESH)
    pl.semaphore_wait(barrier, len(everyone))

    sent = []

    reduce = []
    for d in range(1, GENE):
        copy = remote(
            part_ref.at[pl.ds(pl.multiple_of(genes[d] * piece, piece), piece)],
            arrived.at[d - 1], reduce_send.at[d - 1], reduce_recv.at[d - 1], peers[d - 1],
        )
        copy.start()
        reduce.append(copy)
    grow[cell] = growth_ref[...]
    growth_copy = remote(grow.at[cell], grow.at[cell], grow_send, grow_recv, y_dev)
    growth_copy.start()

    norm_scale = LOG2E / (features * EPSILON)
    weight = weight_ref[...]
    load.wait()

    def norms(step, carry):
        start = pl.multiple_of(step * LANES, LANES)
        norm = scaled_norms(cent[pl.ds(start, LANES), :], norm_scale)
        site_pot[pl.ds(start, LANES), :] = -norm
        norm_out[pl.ds(step, 1), :] = to_row(norm)
        weight_col[pl.ds(start, LANES), :] = to_column(weight_ref[pl.ds(step, 1), :])
        return carry

    lax.fori_loop(0, sites // LANES, norms, 0)
    weight_sum = jnp.sum(jnp.sum(weight, axis=0, keepdims=True), axis=1, keepdims=True)
    weight_row = jnp.broadcast_to(weight_sum, (1, LANES))

    def rows(cell_at, site_at, gene_at):
        at = cell_at * cell_rows + site_at * strip + gene_at * piece
        return proj.at[pl.ds(pl.multiple_of(at, piece), piece)]

    def group(cell_at, site_at):
        at = cell_at * cell_rows + site_at * strip
        return proj.at[pl.ds(pl.multiple_of(at, strip), strip)]

    def send(ref, send_sem, recv_sem, device):
        copy = remote(ref, ref, send_sem, recv_sem, device)
        copy.start()
        sent.append(copy)

    def await_piece(ref, send_sem, recv_sem, device):
        remote(ref, ref, send_sem, recv_sem, device).wait_recv()

    total = part_ref[pl.ds(pl.multiple_of(gene * piece, piece), piece), :]
    for d in range(1, GENE):
        reduce[d - 1].wait_recv()
        total = total + arrived[d - 1]
    own_at = cell * cell_rows + site * strip + gene * piece
    proj[pl.ds(pl.multiple_of(own_at, piece), piece), :] = total.astype(jnp.bfloat16)

    for d in range(1, GENE):
        send(rows(cell, site, gene), z_send.at[d - 1], z_recv.at[d - 1], peers[d - 1])
    for d in range(GENE):
        block = rows(cell, site, back[d])
        if d > 0:
            await_piece(block, z_send.at[d - 1], z_recv.at[d - 1], peers[d - 1])
        send(block, x_send.at[d], x_recv.at[d], x_dev)
        send(block, y_send.at[d], y_recv.at[d], y_dev)
    send(group(cell, site), core_send.at[0], core_recv.at[0], core_dev)
    for d in range(GENE):
        block = rows(cell, x_site, back[d])
        await_piece(block, x_send.at[d], x_recv.at[d], x_dev)
        if d < 2:
            send(block, diag_send.at[d], diag_recv.at[d], y_dev)
        block = rows(other_cell, site, back[d])
        await_piece(block, y_send.at[d], y_recv.at[d], y_dev)
        if d >= 2:
            send(block, diag_send.at[d], diag_recv.at[d], x_dev)
    send(group(cell, x_site), core_send.at[1], core_recv.at[1], core_dev)
    send(group(other_cell, site), core_send.at[2], core_recv.at[2], core_dev)
    scale = 2.0 * norm_scale
    blocks = cells // LANES
    half_blocks = cell_rows // LANES
    bulk = 512
    start_state = (
        jnp.full((8, LANES), -1e38, jnp.float32), jnp.zeros((8, LANES), jnp.float32)
    )

    def await_groups(pairs):
        for at, cell_at, site_at in pairs:
            await_piece(group(cell_at, site_at), core_send.at[at], core_recv.at[at], core_dev)

    def score(cell_at, start):
        side = pl.multiple_of(cell_at * cell_rows, cell_rows)
        scores[start : start + bulk, pl.ds(side, cell_rows)] = scale * lax.dot_general(
            cent[start : start + bulk, :], proj[pl.ds(side, cell_rows), :],
            (((1,), (1,)), ((), ())), preferred_element_type=jnp.float32,
        )

    def add(cell_at, start, states):
        side = pl.multiple_of(cell_at * cell_rows, cell_rows)
        for at in range(start, start + bulk, TALL):
            pot = site_pot[at : at + TALL, :]
            states = tuple(
                fold(scores, pot, at, pl.multiple_of(side + lane * LANES, LANES), states[lane])
                for lane in range(half_blocks)
            )
        return states

    await_groups(((0, cell, core_site), (1, cell, far_site)))
    here = there = (start_state,) * half_blocks
    middle = sites // 2
    score(cell, 0)
    for start in range(bulk, middle, bulk):
        here = add(cell, start - bulk, here)
        score(cell, start)
    for d in range(GENE):
        await_piece(
            rows(other_cell, x_site, back[d]), diag_send.at[d], diag_recv.at[d],
            y_dev if d < 2 else x_dev,
        )
    send(group(other_cell, x_site), core_send.at[3], core_recv.at[3], core_dev)
    for start in range(middle, sites, bulk):
        here = add(cell, start - bulk, here)
        score(cell, start)
    await_groups(((2, other_cell, core_site), (3, other_cell, far_site)))
    here = add(cell, sites - bulk, here)
    score(other_cell, 0)
    for start in range(bulk, sites, bulk):
        there = add(other_cell, start - bulk, there)
        score(other_cell, start)
    there = add(other_cell, sites - bulk, there)
    is_low = cell == 0
    pick = functools.partial(jax.tree.map, lambda p, q: jnp.where(is_low, p, q))
    states = pick(here, there) + pick(there, here)

    def exchange(turn, states):
        closed = [close(state) for state in states]
        peak = jnp.concatenate([pair[0] for pair in closed], axis=1)
        summed = jnp.concatenate([pair[1] for pair in closed], axis=1)
        message[turn, site] = jnp.concatenate([peak, summed, weight_row], axis=1)
        for at, (device, _) in enumerate(site_devs):
            own = message.at[turn, site]
            send(own, lse_send.at[turn, at], lse_recv.at[turn, at], device)
        for at, (device, source) in enumerate(site_devs):
            slot = message.at[turn, source]
            await_piece(slot, lse_send.at[turn, at], lse_recv.at[turn, at], device)
        parts = [message[turn, s] for s in range(SITE)]
        peak = functools.reduce(jnp.maximum, [part[:, :cells] for part in parts])
        summed = sum(part[:, cells : 2 * cells] * jnp.exp2(part[:, :cells] - peak) for part in parts)
        weight_total = sum(part[:, 2 * cells :] for part in parts)
        return peak + jnp.log(summed) * LOG2E, weight_total

    lse, weight_total = exchange(0, states)
    growth_copy.wait_send()
    slot = grow.at[other_cell]
    await_piece(slot, grow_send, grow_recv, y_dev)
    growth = jnp.concatenate([grow[c] for c in range(CELL)], axis=1)
    log_a = jnp.log(growth / jnp.sum(growth, axis=1, keepdims=True)) * LOG2E
    pot = log_a - lse

    rows_at_once = 32

    def repot(start):
        for sub in range(TALL // rows_at_once):
            at = pl.ds(start + sub * rows_at_once, rows_at_once)
            block = scores[at, :] + pot
            peak = jnp.max(block, axis=1, keepdims=True)
            summed = jnp.sum(jnp.exp2(block - peak), axis=1, keepdims=True)
            share = weight_col[at, :] / weight_total
            site_pot[at, :] = jnp.log(share / summed) * LOG2E - peak

    def refold(start, states):
        new = site_pot[pl.ds(start, TALL), :]
        return tuple(
            fold(scores, new, start, lane * LANES, states[lane]) for lane in range(blocks)
        )

    def second(step, states):
        states = refold(pl.multiple_of((step - 1) * TALL, TALL), states)
        repot(pl.multiple_of(step * TALL, TALL))
        return states

    repot(0)
    states = lax.fori_loop(1, sites // TALL, second, (start_state,) * blocks)
    states = refold(sites - TALL, states)
    lse, _ = exchange(1, states)
    pot = log_a - lse

    proj_out[...] = proj[...]
    pot_out[...] = pot
    weight_out[...] = weight_total
    own = proj[pl.ds(pl.multiple_of(cell * cell_rows, cell_rows), cell_rows), :].astype(jnp.float32)
    square = own * own
    high = square.astype(jnp.bfloat16)
    low = (square - high.astype(jnp.float32)).astype(jnp.bfloat16)
    ones = jnp.ones((16, features), jnp.bfloat16)
    norm = sum(
        lax.dot_general(ones, half, (((1,), (1,)), ((), ())), preferred_element_type=jnp.float32)
        for half in (high, low)
    )[:1]
    own_pot = jnp.where(cell == 0, pot[:, :cell_rows], pot[:, cell_rows:])
    cell_out[...] = (EPSILON * LN2) * own_pot + norm * (1.0 / features)
    for copy in sent:
        copy.wait_send()
    for copy in reduce:
        copy.wait_send()


def transport_kernel(
    scores, proj, pot_ref, cell_ref, weight_col, total_ref, norm_ref,
    cell_out, site_out, bary_hbm, coupling, bary, sems,
):
    sites, features = bary.shape
    cells = scores.shape[1]
    rows_at_once = 32
    cell_out[...] = cell_ref[...]
    pot = pot_ref[...]
    weight_total = total_ref[...]

    def couple(chunk):
        slot = chunk % 2
        for base in range(0, TALL, LANES):
            columns = []
            for sub in range(base, base + LANES, rows_at_once):
                at = pl.ds(chunk * TALL + sub, rows_at_once)
                block = scores[at, :] + pot
                peak = jnp.max(block, axis=1, keepdims=True)
                block = jnp.exp2(block - peak)
                summed = jnp.sum(block, axis=1, keepdims=True)
                ratio = weight_col[at, :] / weight_total / summed
                columns.append(jnp.log(ratio) * LOG2E - peak)
                coupling[slot, sub : sub + rows_at_once, :] = (
                    block * tiled(ratio, cells)
                ).astype(jnp.bfloat16)
            row = (chunk * TALL + base) // LANES
            pot_row = to_row(jnp.concatenate(columns, axis=0))
            site_out[row : row + 1, :] = (EPSILON * LN2) * (pot_row + norm_ref[row : row + 1, :])

    def carry(chunk):
        at = pl.ds(chunk * TALL, TALL)
        carried = jnp.dot(coupling[chunk % 2], proj[...], preferred_element_type=jnp.float32)
        bary[at, :] = carried * tiled(weight_total / weight_col[at, :], features)
        copy = pltpu.make_async_copy(bary.at[at], bary_hbm.at[at], sems.at[chunk])
        copy.start()
        return copy

    copies = []
    chunks = sites // TALL
    couple(0)
    for chunk in range(chunks):
        if chunk + 1 < chunks:
            couple(chunk + 1)
        copies.append(carry(chunk))
    for copy in copies:
        copy.wait()


def fused_shards(expr, proj_weight, centroids, growth, site_weight):
    cell_rows, genes = expr.shape
    sites, features = centroids.shape
    strip = cell_rows // SITE
    cells = CELL * cell_rows
    quarter = lax.dynamic_slice(expr, (lax.axis_index("site") * strip, 0), (strip, genes))
    part = jnp.dot(quarter, proj_weight, preferred_element_type=jnp.float32)
    vmem = pl.BlockSpec(memory_space=pltpu.VMEM)
    weight = site_weight.reshape(sites // LANES, LANES)
    dma = pltpu.SemaphoreType.DMA
    proj, pot, cell_pot, total, scores, weight_col, norm = pl.pallas_call(
        prepare_kernel,
        out_shape=(
            jax.ShapeDtypeStruct((cells, features), jnp.bfloat16),
            jax.ShapeDtypeStruct((1, cells), jnp.float32),
            jax.ShapeDtypeStruct((1, cell_rows), jnp.float32),
            jax.ShapeDtypeStruct((1, LANES), jnp.float32),
            jax.ShapeDtypeStruct((sites, cells), jnp.float32),
            jax.ShapeDtypeStruct((sites, LANES), jnp.float32),
            jax.ShapeDtypeStruct((sites // LANES, LANES), jnp.float32),
        ),
        in_specs=[vmem, pl.BlockSpec(memory_space=pl.ANY), vmem, vmem],
        out_specs=(vmem,) * 7,
        scratch_shapes=[
            pltpu.VMEM((sites, features), jnp.bfloat16),
            pltpu.VMEM((GENE - 1, strip // GENE, features), jnp.float32),
            pltpu.VMEM((cells, features), jnp.bfloat16),
            pltpu.VMEM((sites, LANES), jnp.float32),
            pltpu.VMEM((CELL, 1, cell_rows), jnp.float32),
            pltpu.VMEM((ROUNDS, SITE, 1, 2 * cells + LANES), jnp.float32),
            dma, dma((3,)), dma((3,)), dma((3,)), dma((3,)),
            dma((4,)), dma((4,)), dma((4,)), dma((4,)), dma((4,)), dma((4,)), dma((4,)), dma((4,)),
            dma, dma, dma((ROUNDS, 3)), dma((ROUNDS, 3)),
        ],
        compiler_params=pltpu.CompilerParams(
            collective_id=0, has_side_effects=True, vmem_limit_bytes=36 * 1024 * 1024
        ),
        name="prepare",
    )(part, centroids, growth.reshape(1, cell_rows), weight)
    cell_pot, site_pot, barycenter = pl.pallas_call(
        transport_kernel,
        out_shape=(
            jax.ShapeDtypeStruct((1, cell_rows), jnp.float32),
            jax.ShapeDtypeStruct((sites // LANES, LANES), jnp.float32),
            jax.ShapeDtypeStruct((sites, features), jnp.float32),
        ),
        in_specs=[vmem] * 7,
        out_specs=(vmem, vmem, pl.BlockSpec(memory_space=pl.ANY)),
        scratch_shapes=[
            pltpu.VMEM((2, TALL, cells), jnp.bfloat16),
            pltpu.VMEM((sites, features), jnp.float32),
            dma((sites // TALL,)),
        ],
        compiler_params=pltpu.CompilerParams(vmem_limit_bytes=36 * 1024 * 1024),
        name="transport",
    )(scores, proj, pot, cell_pot, weight_col, total, norm)
    return cell_pot.reshape(cell_rows), site_pot.reshape(sites), barycenter


def solution(mesh):
    placed = (P("cell", "gene"), P("gene", None), P("site", None), P("cell"), P("site"))
    sizes = dict(mesh.shape)
    small = sizes["gene"] == 4 and sizes["cell"] == 2 and sizes["site"] == 4
    return jax.shard_map(
        fused_shards if small else shards,
        mesh=mesh,
        in_specs=placed,
        out_specs=(P("cell"), P("site"), P("site", None)),
        check_vma=False,
    )
```
